256 devices in a mesh: group: 16 (over y, z_lo, core), fsdp: 16 (over z_hi, x).
Axes of the slice: x: 4, y: 4, z: 8 (z_hi: 4, z_lo: 2; z = z_hi * 2 + z_lo), core: 2. Of those that a mesh axis runs over, the one named last changes fastest.
Arguments:
- inputs: bfloat16 [16, 4096, 8192], P('group', 'fsdp'), may hold values from -6 to 6
- cotangent: bfloat16 [16, 4096, 512], P('group', 'fsdp'), may hold values from -0.29882812 to 0.29882812
- weight: bfloat16 [16, 8192, 512], P('group', 'fsdp'), may hold values from -6 to 6
- moment: bfloat16 [16, 8192, 512], P('group', 'fsdp'), may hold values from -6 to 6
- second: float32 [16, 8192, 512], P('group', 'fsdp'), may hold values from 0.5 to 4
- step_index: int32 [1], replicated, may hold values from 0 to 999
Outputs:
- input_grad: bfloat16 [16, 4096, 8192], P('group', 'fsdp')
- new_weight: bfloat16 [16, 8192, 512], P('group', 'fsdp')
- new_moment: bfloat16 [16, 8192, 512], P('group', 'fsdp')
- new_second: float32 [16, 8192, 512], P('group', 'fsdp')
The draws below stay inside these ranges and needn't reach their ends.
All inputs are finite; a program needn't handle non-finite values.
Results may differ from the reference program's by a relative error of at most 0.013.
Values may be sent and summed in bfloat16 or wider, within the bound.
No kernel may reach another device: no remote copies, remote signals or barrier semaphores. Data moves between devices by JAX's collectives and lax.ppermute only.
A program may use at most 128 MiB of HBM per device.

```python
import math
import jax
import jax.numpy as jnp
from jax import lax

D = 8192
K = 512
TOKENS = 4096
GROUPS = 16
N_GROUP = 16


def strengthened(values, stream_key, source, target, parts, factor):
    def block_of(dim):
        return (jnp.arange(values.shape[dim]) // (values.shape[dim] // parts)).reshape((-1,) + (1,) * (values.ndim - 1 - dim))

    first = jax.random.permutation(stream_key, parts)[block_of(target)]
    far = (block_of(target) + parts // 2) % parts
    return jnp.where((block_of(source) == first) | (block_of(source) == far), factor * values, values)


def shard_levels(stream_key, dims, pieces, smallest, top_value):
    gain = 1.0
    for position, shards_of in pieces:
        heights = jax.random.uniform(jax.random.fold_in(jax.random.fold_in(stream_key, 6), position), (shards_of,), jnp.float32, smallest / len(pieces), top_value / len(pieces))
        gain = gain * jnp.repeat(jnp.exp(heights), dims[position] // shards_of).reshape((-1,) + (1,) * (len(dims) - 1 - position))
    return gain


def noise(rng, dims, width, reach, cuts=(), kind=jnp.bfloat16):
    values = width * jax.random.normal(rng, dims, jnp.float32)
    if cuts:
        values = values * shard_levels(rng, dims, cuts, -0.22, 0.18)
    return jnp.clip(values, -reach, reach).astype(kind)


def bell_draw_with(own_key, shape, scale, bound, cuts, heavy, kind=jnp.bfloat16):
    result = scale * jax.random.normal(own_key, shape, jnp.float32)
    if cuts:
        result = result * shard_levels(own_key, shape, cuts, -0.22, 0.18)
    return jnp.clip(strengthened(result, jax.random.fold_in(own_key, 3), *heavy), -bound, bound).astype(kind)


def setup_inputs(seed: int = 0) -> dict:
    seeds = jax.random.split(jax.random.key(seed), 7)
    return {
        "inputs": bell_draw_with(seeds[0], (GROUPS, TOKENS, D), 1.0, 6.0, ((0, 16), (1, 16)), (1, 2, 16, 2.0)),
        "cotangent": noise(seeds[1], (GROUPS, TOKENS, K), 0.05, 0.29882812, ((0, 16), (1, 16))),
        "weight": noise(seeds[2], (GROUPS, D, K), 1.0, 6.0, ((0, 16), (1, 16))),
        "moment": noise(seeds[3], (GROUPS, D, K), 1.0, 6.0, ((0, 16), (1, 16))),
        "second": jnp.clip(jnp.exp(math.log(4.0) - 2.0794415 * jax.random.uniform(seeds[4], (GROUPS, D, K), jnp.float32) ** shard_levels(seeds[4], (GROUPS, D, K), ((0, 16), (1, 16)), -0.2, 0.2)), 0.5, 4.0),
        "step_index": jax.random.randint(seeds[5], (1,), 0, 1000).astype(jnp.int32),
    }


def one_group(items):
    inputs, cotangent, weight, moment, second = items
    input_grad = lax.dot_general(cotangent, weight, (((1,), (1,)), ((), ())), preferred_element_type=jnp.float32).astype(jnp.bfloat16)
    gradient = lax.dot_general(inputs, cotangent, (((0,), (0,)), ((), ())), preferred_element_type=jnp.float32)
    first = 0.9 * moment.astype(jnp.float32) + 0.1 * gradient
    new_second = 0.95 * second + 0.05 * gradient * gradient
    weight_f = weight.astype(jnp.float32)
    updated = (weight_f - 0.1 * (first / (jnp.sqrt(new_second) + 1e-08) + 1.0 * weight_f)).astype(jnp.bfloat16)
    return (input_grad, updated, first.astype(jnp.bfloat16), new_second)

def reference(inputs, cotangent, weight, moment, second, step_index):
    nbits = N_GROUP.bit_length() - 1
    input_grad, updated, new_moment, new_second = lax.map(one_group, (inputs, cotangent, weight, moment, second))
    bit = jnp.mod(step_index[0].astype(jnp.int32), jnp.int32(nbits))
    partner = jnp.bitwise_xor(jnp.arange(N_GROUP, dtype=jnp.int32), jnp.left_shift(jnp.int32(1), bit))
    other = updated[partner]
    new_weight = ((updated.astype(jnp.float32) + other.astype(jnp.float32)) * 0.5).astype(jnp.bfloat16)
    return (input_grad, new_weight, new_moment, new_second)
```

```python
from functools import partial

import jax
import jax.numpy as jnp
from jax import lax
from jax.experimental import pallas as pl
from jax.experimental.pallas import tpu as pltpu
from jax.sharding import PartitionSpec as P

X = 4
Z = 4


def moved(v, along, flip, far=False):
    def target(g, f):
        step = 2 if far else 1 if g % 2 == flip else 3
        if along == "x":
            return f // X * X + (f % X + step) % X
        return (f // X + step) % Z * X + f % X

    groups = lax.axis_size("group")
    pairs = [
        (g * X * Z + f, g * X * Z + target(g, f)) for g in range(groups) for f in range(X * Z)
    ]
    return lax.ppermute(v, ("group", "fsdp"), pairs)


def swapped(v, bit):
    return lax.ppermute(
        v, "group", [(i, i ^ 1 << bit) for i in range(lax.axis_size("group"))]
    )


def column(place_ref, zs, xs, depth):
    z, x, up = place_ref[0], place_ref[1], place_ref[2]
    named = {"up": up, "down": 4 - up}
    zs, xs = named.get(zs, zs), named.get(xs, xs)
    block = lax.rem(z + zs, Z) * X + lax.rem(x + xs, X)
    return pl.ds(pl.multiple_of(block * depth, depth), depth)


def carry(copies):
    for copy in copies:
        copy.start()
    for copy in copies:
        copy.wait()


def kernel_call(body, out_shapes, in_specs, out_specs, copies=0, aliases=None, grid=()):
    return pl.pallas_call(
        body,
        grid=grid,
        in_specs=in_specs,
        out_specs=out_specs,
        out_shape=out_shapes,
        scratch_shapes=[pltpu.SemaphoreType.DMA((copies,))] if copies else [],
        input_output_aliases=aliases or {},
        compiler_params=pltpu.CompilerParams(vmem_limit_bytes=16 << 20),
        cost_estimate=pl.CostEstimate(flops=1, bytes_accessed=1, transcendentals=0),
    )


SCALARS = pl.BlockSpec(memory_space=pltpu.SMEM)
THERE = pl.BlockSpec(memory_space=pl.ANY)
HERE = pl.BlockSpec(memory_space=pltpu.VMEM)


def rows_of(n, rows, columns):
    return pl.BlockSpec((rows, columns), lambda i: (n, 0))


def pick_kernel(blocks, place_ref, whole_ref, *refs):
    *tails, out_ref, sems = refs
    depth = out_ref.shape[1]
    tokens = whole_ref.shape[0]
    sources = [whole_ref.at[:, column(place_ref, *b, depth)] for b in blocks] + tails
    carry(
        [
            pltpu.make_async_copy(src, out_ref.at[n * tokens : (n + 1) * tokens], sems.at[n])
            for n, src in enumerate(sources)
        ]
    )


def picked(place, blocks, whole, *tails):
    tokens, width = whole.shape
    count = len(blocks) + len(tails)
    return kernel_call(
        partial(pick_kernel, blocks),
        jax.ShapeDtypeStruct((count * tokens, width // (X * Z)), whole.dtype),
        [SCALARS] + [THERE] * (1 + len(tails)),
        HERE,
        copies=count,
    )(place, whole, *tails)


def place_kernel(blocks, place_ref, part_ref, *refs):
    out_ref, sems = refs[-2:]
    tokens, depth = out_ref.shape[0], part_ref.shape[1]
    carry(
        [
            pltpu.make_async_copy(
                part_ref.at[n * tokens : (n + 1) * tokens],
                out_ref.at[:, column(place_ref, *b, depth)],
                sems.at[n],
            )
            for n, b in enumerate(blocks)
        ]
    )


def placed(place, part, blocks, width, whole=()):
    return kernel_call(
        partial(place_kernel, blocks),
        jax.ShapeDtypeStruct((part.shape[0] // len(blocks), width), part.dtype),
        [SCALARS, HERE] + [THERE] * len(whole),
        THERE,
        copies=len(blocks),
        aliases={2: 0} if whole else None,
    )(place, part, *whole)


def share(parts, ups):
    total = 0.0
    for a, u in zip(parts, ups):
        total += lax.dot_general(
            a[...], u[...], (((0,), (0,)), ((), ())), preferred_element_type=jnp.float32
        )
    return total


def first_kernel(*refs):
    parts, (low_ref, high_ref, own_ref) = refs[: 3 * X], refs[3 * X :]
    ups = parts[2 * X :]
    far = share(parts[:X], ups).astype(low_ref.dtype)
    half = low_ref.shape[0]
    low_ref[...] = far[:half]
    high_ref[...] = far[half:]
    own_ref[...] = share(parts[X : 2 * X], ups)


def first_shares(one):
    tokens, depth, outs = one[0].shape[0] // 3, one[0].shape[1], one[0].shape[1]
    halves = jax.ShapeDtypeStruct((depth // 2, outs), jnp.bfloat16)
    return kernel_call(
        first_kernel,
        (halves, halves, jax.ShapeDtypeStruct((depth, outs), jnp.float32)),
        [rows_of(n, tokens, depth) for n in range(3) for _ in range(X)],
        (HERE,) * 3,
        grid=(1,),
    )(*one, *one, *one)


def second_kernel(*refs):
    parts, (low_ref, high_ref, up_ref, down_ref) = refs[: 3 * X], refs[3 * X :]
    ups = parts[2 * X :]
    half = low_ref.shape[0]
    plus = share(parts[:X], ups)
    up_ref[:half] = (plus[:half] + low_ref[...].astype(jnp.float32)).astype(up_ref.dtype)
    up_ref[half:] = plus[half:].astype(up_ref.dtype)
    minus = share(parts[X : 2 * X], ups)
    down_ref[:half] = minus[:half].astype(down_ref.dtype)
    down_ref[half:] = (minus[half:] + high_ref[...].astype(jnp.float32)).astype(down_ref.dtype)


def second_shares(two, one, low, high):
    tokens, depth, outs = one[0].shape[0] // 3, one[0].shape[1], one[0].shape[1]
    return kernel_call(
        second_kernel,
        (jax.ShapeDtypeStruct((depth, outs), jnp.bfloat16),) * 2,
        [rows_of(n, tokens, depth) for n in range(3) for _ in range(X)] + [HERE] * 2,
        (HERE,) * 2,
        grid=(1,),
    )(*two, *two, *one, low, high)


def rows_kernel(u_ref, *refs):
    *weights, out_ref = refs
    tokens = u_ref.shape[0]
    depth = out_ref.shape[1]
    row = col = 0
    for w in weights:
        out_ref[row : row + tokens, col : col + w.shape[0]] = lax.dot_general(
            u_ref[...], w[...], (((1,), (1,)), ((), ())), preferred_element_type=jnp.float32
        ).astype(out_ref.dtype)
        col += w.shape[0]
        if col == depth:
            row, col = row + tokens, 0


def rows_times(up, *weights):
    tokens, outs = up.shape[0] // 3, up.shape[1]
    depth = weights[0].shape[0]
    return kernel_call(
        rows_kernel,
        jax.ShapeDtypeStruct((tokens * Z, depth), up.dtype),
        [rows_of(2, tokens, outs)] + [HERE] * len(weights),
        HERE,
        grid=(1,),
    )(up, *weights)


class Line:
    def __init__(self):
        self.last = ()

    def __call__(self, *values):
        values, self.last = lax.optimization_barrier((values, self.last))
        self.last = values[:1]
        return values[0] if len(values) == 1 else values

    def run(self, f, *values):
        out = f(*lax.optimization_barrier((values, self.last))[0])
        self.last = (out[0] if isinstance(out, tuple) else out,)
        return out


def local(inputs, cotangent, weight, moment, second, step_index):
    features = inputs[0]
    upstream = cotangent[0]
    rows_here = weight[0]
    tokens, width = features.shape
    depth, outs = rows_here.shape
    me = lax.axis_index("fsdp")
    up = 1 + 2 * (lax.axis_index("group") % 2)
    place = jnp.stack([me // X, me % X, up]).astype(jnp.int32)
    line = Line()
    run = line.run

    def first_part(s):
        return run(lambda f, u: picked(place, [(2, s), (0, s)], f, u), features, upstream)

    def second_part(s):
        return run(lambda f: picked(place, [("up", s), ("down", s)], f), features)

    def long(v):
        return v.astype(jnp.float32)

    def put(s, part, whole=()):
        blocks = [(r, s) for r in (0, "up", "down", 2)]
        return [run(lambda p, *w: placed(place, p, blocks, width, w), part, *whole)]

    half = depth // 2
    above = moved(rows_here, "z", 1)
    below = moved(rows_here, "z", 0)
    c1 = moved(first_part(2), "x", 0, far=True)
    a1 = moved(first_part("up"), "x", 0)
    b1 = moved(first_part("down"), "x", 1)
    own1 = first_part(0)
    own2 = second_part(0)
    c1 = line(c1)
    a2 = moved(second_part("up"), "x", 0)
    above = line(above)
    low = moved(run(lambda v: v[:half], above), "z", 1)
    below = line(below)
    high = moved(run(lambda v: v[half:], below), "z", 0)
    a1 = line(a1)
    b2 = moved(second_part("down"), "x", 1)
    b1 = line(b1)
    c2 = moved(second_part(2), "x", 0, far=True)
    one = (own1, a1, b1, c1)
    far_low, far_high, own = run(lambda *o: first_shares(o), *one)
    low = line(low)
    far_low = moved(far_low, "z", 0)
    high = line(high)
    far_high = moved(far_high, "z", 1)
    rows = (rows_here, above, below, low, high)
    out_c = moved(run(rows_times, c1, *rows), "x", 0, far=True)
    a2 = line(a2)
    out_a = run(rows_times, a1, *rows)
    b2 = line(b2)
    out_b = run(rows_times, b1, *rows)
    far_low = line(far_low)
    far_high = line(far_high)
    input_grad = put(0, run(rows_times, own1, *rows))
    c2 = line(c2)
    two = (own2, a2, b2, c2)
    near_up, near_down = run(
        lambda *v: second_shares(v[:X], v[X : 2 * X], *v[2 * X :]), *two, *one, far_low, far_high
    )
    near_up = moved(near_up, "z", 0)
    near_down = moved(near_down, "z", 1)
    out_a = moved(out_a, "x", 1)
    out_b = moved(out_b, "x", 0)
    out_c = line(out_c)
    input_grad = put(2, out_c, input_grad)
    near_up = line(near_up)
    near_down = line(near_down)
    gradient = own + long(near_up) + long(near_down)

    first = 0.9 * moment[0].astype(jnp.float32) + 0.1 * gradient
    new_second = 0.95 * second[0] + 0.05 * gradient * gradient
    weight_f = rows_here.astype(jnp.float32)
    updated = (weight_f - 0.1 * (first / (jnp.sqrt(new_second) + 1e-08) + 1.0 * weight_f)).astype(
        jnp.bfloat16
    )
    nbits = lax.axis_size("group").bit_length() - 1
    chosen = jnp.mod(step_index[0], nbits)
    partner_rows = lax.switch(chosen, [partial(swapped, bit=b) for b in range(nbits)], updated)
    new_weight = ((updated.astype(jnp.float32) + partner_rows.astype(jnp.float32)) * 0.5).astype(
        jnp.bfloat16
    )
    new_weight = line(new_weight)
    out_a = line(out_a)
    input_grad = put("up", out_a, input_grad)
    out_b = line(out_b)
    input_grad = put("down", out_b, input_grad)[0]
    return (input_grad[None], new_weight[None], first.astype(jnp.bfloat16)[None], new_second[None])


def solution(mesh):
    sharded = P("group", "fsdp", None)
    return jax.shard_map(
        local,
        mesh=mesh,
        in_specs=(sharded,) * 5 + (P(),),
        out_specs=(sharded,) * 4,
        check_vma=False,
    )
```

```python
from functools import partial

import jax
import jax.numpy as jnp
from jax import lax
from jax.experimental import pallas as pl
from jax.experimental.pallas import tpu as pltpu
from jax.sharding import PartitionSpec as P

X = 4
Z = 4


def moved(v, along, flip=0):
    def target(g, f):
        z, x = f // X, f % X
        if along == "x":
            x = partners(g, x)[flip]
        else:
            z = (z + (1 if g % 2 == flip else 3)) % Z
        return z * X + x

    groups = lax.axis_size("group")
    pairs = [
        (g * X * Z + f, g * X * Z + target(g, f)) for g in range(groups) for f in range(X * Z)
    ]
    return lax.ppermute(v, ("group", "fsdp"), pairs)


def partners(g, x):
    ways = (x ^ 1, 3 - x)
    return ways if g % 2 == 0 else ways[::-1]


def swapped(v, bit):
    return lax.ppermute(
        v, "group", [(i, i ^ 1 << bit) for i in range(lax.axis_size("group"))]
    )


HERE_X, FIRST, SECOND, BOTH = 2, 3, 4, 5


def column(place_ref, zs, xs, depth):
    z, up = place_ref[0], place_ref[1]
    zs = {"up": up, "down": 4 - up}.get(zs, zs)
    block = lax.rem(z + zs, Z) * X + place_ref[xs]
    return pl.ds(pl.multiple_of(block * depth, depth), depth)


def carry(copies):
    for copy in copies:
        copy.start()
    for copy in copies:
        copy.wait()


def kernel_call(body, out_shapes, in_specs, out_specs, copies=0, aliases=None, cost=1):
    return pl.pallas_call(
        body,
        in_specs=in_specs,
        out_specs=out_specs,
        out_shape=out_shapes,
        scratch_shapes=[pltpu.SemaphoreType.DMA((copies,))] if copies else [],
        input_output_aliases=aliases or {},
        compiler_params=pltpu.CompilerParams(vmem_limit_bytes=16 << 20),
        cost_estimate=pl.CostEstimate(flops=cost, bytes_accessed=cost, transcendentals=0),
    )


SCALARS = pl.BlockSpec(memory_space=pltpu.SMEM)
THERE = pl.BlockSpec(memory_space=pl.ANY)
HERE = pl.BlockSpec(memory_space=pltpu.VMEM)


def pick_kernel(blocks, place_ref, whole_ref, *refs):
    *tails, out_ref, sems = refs
    depth = out_ref.shape[1]
    tokens = whole_ref.shape[0]
    sources = [whole_ref.at[:, column(place_ref, *b, depth)] for b in blocks] + tails
    carry(
        [
            pltpu.make_async_copy(src, out_ref.at[n * tokens : (n + 1) * tokens], sems.at[n])
            for n, src in enumerate(sources)
        ]
    )


def picked(place, blocks, whole, *tails, cost=1):
    tokens, width = whole.shape
    count = len(blocks) + len(tails)
    return kernel_call(
        partial(pick_kernel, blocks),
        jax.ShapeDtypeStruct((count * tokens, width // (X * Z)), whole.dtype),
        [SCALARS] + [THERE] * (1 + len(tails)),
        HERE,
        copies=count,
        cost=cost,
    )(place, whole, *tails)


def placing(blocks, place_ref, parts, out_ref, sems):
    tokens, depth = out_ref.shape[0], parts[0].shape[1]
    copies = []
    for part_ref, some in zip(parts, blocks):
        for n, b in enumerate(some):
            copies.append(
                pltpu.make_async_copy(
                    part_ref.at[n * tokens : (n + 1) * tokens],
                    out_ref.at[:, column(place_ref, *b, depth)],
                    sems.at[len(copies)],
                )
            )
    return copies


def place_kernel(blocks, place_ref, *refs):
    parts, (out_ref, sems) = refs[: len(blocks)], refs[-2:]
    carry(placing(blocks, place_ref, parts, out_ref, sems))


def placed(place, parts, blocks, width, whole=()):
    return kernel_call(
        partial(place_kernel, blocks),
        jax.ShapeDtypeStruct((parts[0].shape[0] // len(blocks[0]), width), parts[0].dtype),
        [SCALARS] + [HERE] * len(parts) + [THERE] * len(whole),
        THERE,
        copies=sum(map(len, blocks)),
        aliases={1 + len(parts): 0} if whole else None,
    )(place, *parts, *whole)


def product_kernel(a_ref, b_ref, u_ref, v_ref, *out_refs):
    tokens = u_ref.shape[0] // 5
    for n, out_ref in enumerate(out_refs):
        total = 0.0
        for p, w in ((a_ref, u_ref), (b_ref, v_ref)):
            total += lax.dot_general(
                p[n * tokens : (n + 1) * tokens],
                w[4 * tokens :],
                (((0,), (0,)), ((), ())),
                preferred_element_type=jnp.float32,
            )
        out_ref[...] = total.astype(out_ref.dtype)


def products(own, came, own_first, came_first):
    depth, outs = own.shape[1], own_first.shape[1]
    return kernel_call(
        product_kernel,
        tuple(jax.ShapeDtypeStruct((depth, outs), t) for t in (jnp.float32, jnp.bfloat16) * 2),
        [HERE] * 4,
        (HERE,) * 4,
    )(own, came, own_first, came_first)


def rows_kernel(u_ref, v_ref, *refs):
    *weights, out_ref, own_ref = refs
    tokens = u_ref.shape[0] // 5
    for first_ref, to_ref in ((u_ref, out_ref), (v_ref, own_ref)):
        for n, w in enumerate(weights):
            to_ref[n * tokens : (n + 1) * tokens] = lax.dot_general(
                first_ref[4 * tokens :],
                w[...],
                (((1,), (1,)), ((), ())),
                preferred_element_type=jnp.float32,
            ).astype(to_ref.dtype)


def rows_times(first, own_first, *weights):
    tokens, depth = first.shape[0] // 5, first.shape[1]
    out = jax.ShapeDtypeStruct((tokens * len(weights), depth), first.dtype)
    return kernel_call(rows_kernel, (out, out), [HERE] * (2 + len(weights)), (HERE, HERE))(
        first, own_first, *weights
    )


class Line:
    def __init__(self):
        self.last = ()

    def __call__(self, *values):
        values, self.last = lax.optimization_barrier((values, self.last))
        self.last = values[:1]
        return values[0] if len(values) == 1 else values

    def run(self, f, *values):
        out = f(*lax.optimization_barrier((values, self.last))[0])
        self.last = (out[0] if isinstance(out, tuple) else out,)
        return out


def local(inputs, cotangent, weight, moment, second, step_index):
    features = inputs[0]
    upstream = cotangent[0]
    rows_here = weight[0]
    tokens, width = features.shape
    depth, outs = rows_here.shape
    me = lax.axis_index("fsdp")
    z, x = me // X, me % X
    odd = lax.axis_index("group") % 2
    one_way, other_way = x ^ 1, 3 - x
    place = [z, 1 + 2 * odd, x]
    place += [jnp.where(odd == 0, one_way, other_way), jnp.where(odd == 0, other_way, one_way)]
    place = jnp.stack(place + [x ^ 2]).astype(jnp.int32)
    line = Line()
    run = line.run

    def first_part(*ways):
        blocks = [(r, w) for r in (2, "up") for w in ways]
        return run(lambda f, u: picked(place, blocks, f, u), features, upstream)

    def second_part(*ways, cost=1):
        blocks = [(r, w) for r in ("down", 0) for w in ways]
        return run(lambda f: picked(place, blocks, f, cost=cost), features)

    def long(v):
        return v.astype(jnp.float32)

    def put(parts, whole=()):
        blocks = [[(r, x) for r in zs] for _, zs, x in parts]
        n = len(parts)
        return [
            run(
                lambda *p: placed(place, p[:n], blocks, width, p[n:]),
                *[part for part, _, _ in parts],
                *whole,
            )
        ]

    def added(a, *v):
        return sum(map(long, v), a).astype(jnp.bfloat16)

    def queued(v):
        return run(lambda w: w, v)

    near, rest = (0, "up"), ("down", 2)

    above = moved(rows_here, "z", 1)
    below = moved(rows_here, "z", 0)
    first = moved(first_part(FIRST, BOTH), "x")
    second_in = moved(second_part(FIRST, BOTH), "x")
    own_first = first_part(HERE_X, SECOND)
    above = line(above)
    below = line(below)
    across = moved(queued(above), "z", 1)
    own_second = second_part(HERE_X, SECOND, cost=10**11)
    first = line(first)
    far, give_far, up, give_up = run(lambda a, b: products(a, b, a, b), own_first, first)
    give_far = moved(give_far, "x", 1)
    give_up = moved(give_up, "x", 1)
    out_near, own_near = run(rows_times, first, own_first, rows_here, above)
    out_near = moved(out_near, "x")
    give_far = line(give_far)
    far = moved(run(added, far, give_far), "z", 0)
    second_in = line(second_in)
    down, give_down, own, give_own = run(products, own_second, second_in, own_first, first)
    give_down = moved(give_down, "x", 1)
    across = line(across)
    give_own = moved(give_own, "x", 1)
    give_up = line(give_up)
    there = moved(rows_here, "x", 1)
    out_rest, own_rest = run(rows_times, first, own_first, below, across)
    out_near = line(out_near)
    there_above = moved(above, "x", 1)
    input_grad = put(
        [(own_near, near, HERE_X), (own_rest, rest, HERE_X), (out_near, near, FIRST)]
    )
    give_down = line(give_down)
    near_down = moved(run(added, down, give_down), "z", 1)
    give_own = line(give_own)
    far = line(far)
    near_up = moved(run(added, up, give_up, far), "z", 0)
    there_below = moved(below, "x", 1)
    there = line(there)
    there_across = moved(across, "x", 1)
    there_above = line(there_above)
    more_near, own_more_near = run(rows_times, first, own_first, there, there_above)
    input_grad = put([(own_more_near, near, SECOND)], input_grad)
    there_below = line(there_below)
    there_across = line(there_across)
    out_rest = moved(queued(out_rest), "x")
    more_near = moved(queued(more_near), "x")
    more_rest, own_more_rest = run(
        rows_times, first, own_first, there_below, there_across
    )
    more_rest = moved(more_rest, "x")
    near_up = line(near_up)
    near_down = line(near_down)
    gradient = own + long(give_own) + long(near_up) + long(near_down)
    new_moment = 0.9 * moment[0].astype(jnp.float32) + 0.1 * gradient
    new_second = 0.95 * second[0] + 0.05 * gradient * gradient
    weight_f = rows_here.astype(jnp.float32)
    updated = (
        weight_f - 0.1 * (new_moment / (jnp.sqrt(new_second) + 1e-08) + 1.0 * weight_f)
    ).astype(jnp.bfloat16)
    new_moment = new_moment.astype(jnp.bfloat16)
    nbits = lax.axis_size("group").bit_length() - 1
    chosen = jnp.mod(step_index[0], nbits)
    partner_rows = lax.switch(chosen, [partial(swapped, bit=b) for b in range(nbits)], updated)
    partner_rows = line(partner_rows)
    new_weight = ((updated.astype(jnp.float32) + partner_rows.astype(jnp.float32)) * 0.5).astype(
        jnp.bfloat16
    )
    new_weight = line(new_weight)
    out_rest, more_near, more_rest = line(out_rest, more_near, more_rest)
    input_grad = put(
        [
            (own_more_rest, rest, SECOND),
            (out_rest, rest, FIRST),
            (more_near, near, BOTH),
            (more_rest, rest, BOTH),
        ],
        input_grad,
    )[0]
    return (input_grad[None], new_weight[None], new_moment[None], new_second[None])


def solution(mesh):
    sharded = P("group", "fsdp", None)
    return jax.shard_map(
        local,
        mesh=mesh,
        in_specs=(sharded,) * 5 + (P(),),
        out_specs=(sharded,) * 4,
        check_vma=False,
    )
```

```python
from functools import partial

import jax
import jax.numpy as jnp
from jax import lax
from jax.experimental import pallas as pl
from jax.experimental.pallas import tpu as pltpu
from jax.sharding import PartitionSpec as P

X = 4
Z = 4


def moved(v, along, flip=0):
    def target(g, f):
        z, x = f // X, f % X
        if along == "x":
            x = partners(g, x)[flip]
        else:
            z = (z + (1 if g % 2 == flip else 3)) % Z
        return z * X + x

    groups = lax.axis_size("group")
    pairs = [
        (g * X * Z + f, g * X * Z + target(g, f)) for g in range(groups) for f in range(X * Z)
    ]
    return lax.ppermute(v, ("group", "fsdp"), pairs)


def partners(g, x):
    ways = (x ^ 1, 3 - x)
    return ways if g % 2 == 0 else ways[::-1]


def swapped(v, bit):
    return lax.ppermute(
        v, "group", [(i, i ^ 1 << bit) for i in range(lax.axis_size("group"))]
    )


HERE_X, FIRST, SECOND, BOTH = 2, 3, 4, 5


def column(place_ref, zs, xs, depth):
    z, up = place_ref[0], place_ref[1]
    zs = {"up": up, "down": 4 - up}.get(zs, zs)
    block = lax.rem(z + zs, Z) * X + place_ref[xs]
    return pl.ds(pl.multiple_of(block * depth, depth), depth)


def carry(copies):
    for copy in copies:
        copy.start()
    for copy in copies:
        copy.wait()


def kernel_call(body, out_shapes, in_specs, out_specs, copies=0, aliases=None, cost=1):
    return pl.pallas_call(
        body,
        in_specs=in_specs,
        out_specs=out_specs,
        out_shape=out_shapes,
        scratch_shapes=[pltpu.SemaphoreType.DMA((copies,))] if copies else [],
        input_output_aliases=aliases or {},
        compiler_params=pltpu.CompilerParams(vmem_limit_bytes=16 << 20),
        cost_estimate=pl.CostEstimate(flops=cost, bytes_accessed=cost, transcendentals=0),
    )


SCALARS = pl.BlockSpec(memory_space=pltpu.SMEM)
THERE = pl.BlockSpec(memory_space=pl.ANY)
HERE = pl.BlockSpec(memory_space=pltpu.VMEM)


def pick_kernel(blocks, place_ref, whole_ref, *refs):
    *tails, out_ref, sems = refs
    depth = out_ref.shape[1]
    tokens = whole_ref.shape[0]
    sources = [whole_ref.at[:, column(place_ref, *b, depth)] for b in blocks] + tails
    carry(
        [
            pltpu.make_async_copy(src, out_ref.at[n * tokens : (n + 1) * tokens], sems.at[n])
            for n, src in enumerate(sources)
        ]
    )


def picked(place, blocks, whole, *tails, cost=1):
    tokens, width = whole.shape
    count = len(blocks) + len(tails)
    return kernel_call(
        partial(pick_kernel, blocks),
        jax.ShapeDtypeStruct((count * tokens, width // (X * Z)), whole.dtype),
        [SCALARS] + [THERE] * (1 + len(tails)),
        HERE,
        copies=count,
        cost=cost,
    )(place, whole, *tails)


def placing(blocks, place_ref, parts, out_ref, sems):
    tokens, depth = out_ref.shape[0], parts[0].shape[1]
    copies = []
    for part_ref, some in zip(parts, blocks):
        for n, b in enumerate(some):
            copies.append(
                pltpu.make_async_copy(
                    part_ref.at[n * tokens : (n + 1) * tokens],
                    out_ref.at[:, column(place_ref, *b, depth)],
                    sems.at[len(copies)],
                )
            )
    return copies


def place_kernel(blocks, place_ref, *refs):
    parts, (out_ref, sems) = refs[: len(blocks)], refs[-2:]
    carry(placing(blocks, place_ref, parts, out_ref, sems))


def placed(place, parts, blocks, width, whole=()):
    return kernel_call(
        partial(place_kernel, blocks),
        jax.ShapeDtypeStruct((parts[0].shape[0] // len(blocks[0]), width), parts[0].dtype),
        [SCALARS] + [HERE] * len(parts) + [THERE] * len(whole),
        THERE,
        copies=sum(map(len, blocks)),
        aliases={1 + len(parts): 0} if whole else None,
    )(place, *parts, *whole)


def product_kernel(a_ref, b_ref, u_ref, v_ref, *out_refs):
    tokens = u_ref.shape[0] // 5
    for n, out_ref in enumerate(out_refs):
        total = 0.0
        for p, w in ((a_ref, u_ref), (b_ref, v_ref)):
            total += lax.dot_general(
                p[n * tokens : (n + 1) * tokens],
                w[4 * tokens :],
                (((0,), (0,)), ((), ())),
                preferred_element_type=jnp.float32,
            )
        out_ref[...] = total.astype(out_ref.dtype)


def products(own, came, own_first, came_first):
    depth, outs = own.shape[1], own_first.shape[1]
    return kernel_call(
        product_kernel,
        tuple(jax.ShapeDtypeStruct((depth, outs), t) for t in (jnp.float32, jnp.bfloat16) * 2),
        [HERE] * 4,
        (HERE,) * 4,
    )(own, came, own_first, came_first)


def rows_kernel(u_ref, v_ref, *refs):
    *weights, out_ref, own_ref = refs
    tokens = u_ref.shape[0] // 5
    for first_ref, to_ref in ((u_ref, out_ref), (v_ref, own_ref)):
        for n, w in enumerate(weights):
            to_ref[n * tokens : (n + 1) * tokens] = lax.dot_general(
                first_ref[4 * tokens :],
                w[...],
                (((1,), (1,)), ((), ())),
                preferred_element_type=jnp.float32,
            ).astype(to_ref.dtype)


def rows_times(first, own_first, *weights):
    tokens, depth = first.shape[0] // 5, first.shape[1]
    out = jax.ShapeDtypeStruct((tokens * len(weights), depth), first.dtype)
    return kernel_call(rows_kernel, (out, out), [HERE] * (2 + len(weights)), (HERE, HERE))(
        first, own_first, *weights
    )


class Line:
    def __init__(self):
        self.last = ()

    def __call__(self, *values):
        values, self.last = lax.optimization_barrier((values, self.last))
        self.last = values[:1]
        return values[0] if len(values) == 1 else values

    def run(self, f, *values):
        out = f(*lax.optimization_barrier((values, self.last))[0])
        self.last = (out[0] if isinstance(out, tuple) else out,)
        return out


def local(inputs, cotangent, weight, moment, second, step_index):
    features = inputs[0]
    upstream = cotangent[0]
    rows_here = weight[0]
    tokens, width = features.shape
    depth, outs = rows_here.shape
    me = lax.axis_index("fsdp")
    z, x = me // X, me % X
    odd = lax.axis_index("group") % 2
    one_way, other_way = x ^ 1, 3 - x
    place = [z, 1 + 2 * odd, x]
    place += [jnp.where(odd == 0, one_way, other_way), jnp.where(odd == 0, other_way, one_way)]
    place = jnp.stack(place + [x ^ 2]).astype(jnp.int32)
    line = Line()
    run = line.run

    def first_part(*ways):
        blocks = [(r, w) for r in (2, "up") for w in ways]
        return run(lambda f, u: picked(place, blocks, f, u), features, upstream)

    def second_part(*ways, cost=1):
        blocks = [(r, w) for r in ("down", 0) for w in ways]
        return run(lambda f: picked(place, blocks, f, cost=cost), features)

    def long(v):
        return v.astype(jnp.float32)

    def put(parts, whole=()):
        blocks = [[(r, x) for r in zs] for _, zs, x in parts]
        n = len(parts)
        return [
            run(
                lambda *p: placed(place, p[:n], blocks, width, p[n:]),
                *[part for part, _, _ in parts],
                *whole,
            )
        ]

    def added(a, *v):
        return sum(map(long, v), a).astype(jnp.bfloat16)

    def queued(v):
        return run(lambda w: w, v)

    near, rest = (0, "up"), ("down", 2)

    above = moved(rows_here, "z", 1)
    below = moved(rows_here, "z", 0)
    first = moved(first_part(FIRST, BOTH), "x")
    second_in = moved(second_part(FIRST, BOTH), "x")
    own_first = first_part(HERE_X, SECOND)
    above = line(above)
    below = line(below)
    across = moved(queued(above), "z", 1)
    own_second = second_part(HERE_X, SECOND, cost=10**11)
    first = line(first)
    far, give_far, up, give_up = run(lambda a, b: products(a, b, a, b), own_first, first)
    give_far = moved(give_far, "x", 1)
    give_up = moved(give_up, "x", 1)
    out_near, own_near = run(rows_times, first, own_first, rows_here, above)
    out_near = moved(out_near, "x")
    give_far = line(give_far)
    far = moved(run(added, far, give_far), "z", 0)
    second_in = line(second_in)
    down, give_down, own, give_own = run(products, own_second, second_in, own_first, first)
    give_down = moved(give_down, "x", 1)
    across = line(across)
    give_own = moved(give_own, "x", 1)
    give_up = line(give_up)
    there = moved(rows_here, "x", 1)
    out_rest, own_rest = run(rows_times, first, own_first, below, across)
    out_near = line(out_near)
    there_above = moved(above, "x", 1)
    give_down = line(give_down)
    near_down = moved(run(added, down, give_down), "z", 1)
    give_own = line(give_own)
    far = line(far)
    near_up = moved(run(added, up, give_up, far), "z", 0)
    there_below = moved(below, "x", 1)
    there = line(there)
    there_across = moved(across, "x", 1)
    input_grad = put(
        [(own_near, near, HERE_X), (own_rest, rest, HERE_X), (out_near, near, FIRST)]
    )
    there_above = line(there_above)
    own = run(lambda a, b: a + long(b), own, give_own)
    more_near, own_more_near = run(rows_times, first, own_first, there, there_above)
    input_grad = put([(own_more_near, near, SECOND)], input_grad)
    there_below = line(there_below)
    there_across = line(there_across)
    out_rest = moved(queued(out_rest), "x")
    more_near = moved(queued(more_near), "x")
    more_rest, own_more_rest = run(
        rows_times, first, own_first, there_below, there_across
    )
    more_rest = moved(more_rest, "x")
    near_up = line(near_up)
    near_down = line(near_down)
    gradient = own + long(near_up) + long(near_down)
    new_moment = 0.9 * moment[0].astype(jnp.float32) + 0.1 * gradient
    new_second = 0.95 * second[0] + 0.05 * gradient * gradient
    weight_f = rows_here.astype(jnp.float32)
    updated = (
        weight_f - 0.1 * (new_moment / (jnp.sqrt(new_second) + 1e-08) + 1.0 * weight_f)
    ).astype(jnp.bfloat16)
    new_moment = new_moment.astype(jnp.bfloat16)
    nbits = lax.axis_size("group").bit_length() - 1
    chosen = jnp.mod(step_index[0], nbits)
    partner_rows = lax.switch(chosen, [partial(swapped, bit=b) for b in range(nbits)], updated)
    partner_rows = line(partner_rows)
    new_weight = ((updated.astype(jnp.float32) + partner_rows.astype(jnp.float32)) * 0.5).astype(
        jnp.bfloat16
    )
    new_weight = line(new_weight)
    out_rest, more_near, more_rest = line(out_rest, more_near, more_rest)
    input_grad = put(
        [
            (own_more_rest, rest, SECOND),
            (out_rest, rest, FIRST),
            (more_near, near, BOTH),
            (more_rest, rest, BOTH),
        ],
        input_grad,
    )[0]
    return (input_grad[None], new_weight[None], new_moment[None], new_second[None])


def solution(mesh):
    sharded = P("group", "fsdp", None)
    return jax.shard_map(
        local,
        mesh=mesh,
        in_specs=(sharded,) * 5 + (P(),),
        out_specs=(sharded,) * 4,
        check_vma=False,
    )
```
